512 devices in a mesh: node: 8 (over y, core), scen: 64 (over z, x).
Axes of the slice: x: 4, y: 4, z: 16, core: 2. Of those that a mesh axis runs over, the one named last changes fastest.
Arguments:
- sample_submatrices: bfloat16 [8192, 128, 1024], P(('node', 'scen')), may hold values from -0.176776695 to 0.176776695
- penalty_weights: float32 [8192, 128], P(('node', 'scen')), may hold values from 0.001 to 10
- sample_patch_pattern: int32 [8192, 8], P(('node', 'scen')), may hold values 0 or 1
- terminal_penalty_entries: float32 [8, 1024], P('node'), may hold values from 0.25 to 4
- terminal_ancestor_coupler: bfloat16 [8, 1024, 256], P('node'), may hold values from -0.1875 to 0.1875
- secondary_penalty_entries: float32 [2, 256], replicated, may hold values from 0.25 to 4
- secondary_base_coupler: bfloat16 [2, 256, 128], replicated, may hold values from -0.375 to 0.375
- opening_penalty_entries: float32 [128], replicated, may hold values from 0.25 to 4
Outputs:
- node_factor: float32 [8, 1024, 1024], P('node', 'scen')
- parent_factor: float32 [2, 256, 256], replicated
- root_factor: float32 [128, 128], replicated
The draws below stay inside these ranges and needn't reach their ends.
All inputs are finite; a program needn't handle non-finite values. No bound on the sum of `sample_patch_pattern` on one device may be relied on, other than what follows from the above.
Results may differ from the reference program's by a relative error of at most 0.00037.
Values sent between devices are 32-bit elements; how exact they have to be, the bound alone decides.
No kernel may reach another device: no remote copies, remote signals or barrier semaphores. Data moves between devices by JAX's collectives and lax.ppermute only.
A program may use at most 128 MiB of HBM per device.

```python
import math
import jax
import jax.numpy as jnp
from jax import lax

K = 1024
NTILE = 8
COUPLER_LINES = 128
UNIT_SAMPLES = 16
P_SIZE = 256
R = 128
PARENTS = 2
TERTIARY_POINTS = 8
SAMPLE_TOTAL = 8192
GROUP_ROWS = 131072
N_SCEN = 64


def draw_sample_submatrices(key, part):
    key = jax.random.fold_in(key, 11)
    keys = jax.random.split(key, 5)
    sigma = GROUP_ROWS ** (-0.5)
    shape = (SAMPLE_TOTAL, COUPLER_LINES, K)
    noise = jax.random.truncated_normal(keys[0], -6.0, 6.0, shape, jnp.float32)
    row_scale = jnp.ones((SAMPLE_TOTAL, COUPLER_LINES, 1), jnp.float32)
    common_share = 0.17
    block_width = K // N_SCEN
    pairing = jax.vmap(lambda sub: jax.random.permutation(sub, N_SCEN))(jax.random.split(keys[2], TERTIARY_POINTS)).astype(jnp.int32)
    device_ids = jnp.arange(SAMPLE_TOTAL, dtype=jnp.int32) // UNIT_SAMPLES
    target = pairing[device_ids // N_SCEN, device_ids % N_SCEN]
    column_block = jnp.arange(K, dtype=jnp.int32) // block_width
    boost = jnp.where(column_block[None, :] == target[:, None], 5.0, 1.0).astype(jnp.float32)
    common_row = jax.random.truncated_normal(keys[3], -4.0, 4.0, (SAMPLE_TOTAL, COUPLER_LINES, 1), jnp.float32)
    common_col = jax.random.uniform(keys[4], (1, 1, K), jnp.float32, 0.4, 1.6)
    values = sigma * row_scale * (noise * boost[:, None, :] + common_share * common_row * common_col)
    return values.astype(jnp.bfloat16)


def with_ends(array, own_key, low, high):
    place = [jax.random.randint(jax.random.fold_in(own_key, axis), (), 0, length) for axis, length in enumerate(array.shape)]
    widest = array.shape.index(max(array.shape))
    neighbour = place[:widest] + [(place[widest] + 1) % array.shape[widest]] + place[widest + 1:]
    return array.at[tuple(place)].set(low).at[tuple(neighbour)].set(high)


def steps_of(key, extent, shards, low, top_value):
    def one(axis_at, parts):
        draws = jax.random.uniform(jax.random.fold_in(jax.random.fold_in(key, 6), axis_at), (parts,), jnp.float32, low / len(shards), top_value / len(shards))
        return jnp.repeat(jnp.exp(draws), extent[axis_at] // parts).reshape((-1,) + (1,) * (len(extent) - axis_at - 1))

    level = one(*shards[0])
    for cut in shards[1:]:
        level = level * one(*cut)
    return level


def normal_values(key, dims, spread, limit, shards=(), kind=jnp.bfloat16):
    array = spread * jax.random.normal(key, dims, jnp.float32)
    if shards:
        array = array * steps_of(key, dims, shards, -0.22, 0.18)
    return jnp.clip(array, -limit, limit).astype(kind)


def setup_inputs(seed: int = 0) -> dict:
    key_of = jax.random.split(jax.random.key(seed), 9)
    return {
        "sample_submatrices": draw_sample_submatrices(jax.random.fold_in(key_of[8], 71), 0),
        "penalty_weights": jnp.clip(jnp.exp(math.log(10.0) - 9.2103403 * jax.random.uniform(key_of[1], (SAMPLE_TOTAL, COUPLER_LINES), jnp.float32) ** steps_of(key_of[1], (SAMPLE_TOTAL, COUPLER_LINES), ((0, 512),), -0.2, 0.2)), 0.001, 10.0),
        "sample_patch_pattern": with_ends((jax.random.randint(key_of[2], (SAMPLE_TOTAL, NTILE), 0, 2) < 1).astype(jnp.int32), jax.random.fold_in(key_of[2], 1), 0, 1),
        "terminal_penalty_entries": jnp.clip(jnp.exp(math.log(4.0) - 2.7725887 * jax.random.uniform(key_of[3], (TERTIARY_POINTS, K), jnp.float32) ** steps_of(key_of[3], (TERTIARY_POINTS, K), ((0, 8),), -0.2, 0.2)), 0.25, 4.0),
        "terminal_ancestor_coupler": normal_values(key_of[4], (TERTIARY_POINTS, K, P_SIZE), K ** -0.5, 0.1875, ((0, 8),)),
        "secondary_penalty_entries": jnp.clip(jnp.exp(jax.random.uniform(key_of[5], (PARENTS, P_SIZE), jnp.float32, math.log(0.25), math.log(4.0))), 0.25, 4.0),
        "secondary_base_coupler": normal_values(key_of[6], (PARENTS, P_SIZE, R), P_SIZE ** -0.5, 0.375),
        "opening_penalty_entries": jnp.clip(jnp.exp(jax.random.uniform(key_of[7], (R,), jnp.float32, math.log(0.25), math.log(4.0))), 0.25, 4.0),
    }


def column_mask(sample_patch_pattern, width):
    size = width // sample_patch_pattern.shape[1]
    return jnp.repeat(sample_patch_pattern.astype(jnp.float32), size, axis=1)

def weighted_lines(sample_submatrices, penalty_weights, sample_patch_pattern):
    width = sample_submatrices.shape[2]
    patch_field_pattern = column_mask(sample_patch_pattern, width)
    midpoint_extent = sample_submatrices.astype(jnp.float32) * jnp.sqrt(penalty_weights)[:, :, None] * patch_field_pattern[:, None, :]
    return midpoint_extent.astype(jnp.bfloat16).reshape(-1, width)

def node_work(inputs):
    node_blocks, node_scal, node_mask, diag_one, link_one = inputs
    width = node_blocks.shape[3]

    def accumulate(total, piece):
        midpoint_extent = weighted_lines(piece[0], piece[1], piece[2])
        term = lax.dot_general(midpoint_extent.astype(jnp.float32), midpoint_extent.astype(jnp.float32), (((0,), (0,)), ((), ())), preferred_element_type=jnp.float32)
        return (total + term, None)
    start = jnp.zeros((width, width), jnp.float32)
    schur, unused = lax.scan(accumulate, start, (node_blocks, node_scal, node_mask))
    block = schur + jnp.diag(diag_one)
    factor = jnp.linalg.cholesky(block)
    reduced = jax.scipy.linalg.solve_triangular(factor, link_one.astype(jnp.float32), lower=True)
    condensed = jnp.dot(reduced.T, reduced, precision=lax.Precision.HIGHEST)
    return (factor, condensed)

def reference(sample_submatrices, penalty_weights, sample_patch_pattern, terminal_penalty_entries, terminal_ancestor_coupler, secondary_penalty_entries, secondary_base_coupler, opening_penalty_entries):
    width = sample_submatrices.shape[2]
    submatrix_lines = sample_submatrices.shape[1]
    grouped = sample_submatrices.reshape(TERTIARY_POINTS, N_SCEN, UNIT_SAMPLES, submatrix_lines, width)
    factors_bundled = penalty_weights.reshape(TERTIARY_POINTS, N_SCEN, UNIT_SAMPLES, submatrix_lines)
    mask_grouped = sample_patch_pattern.reshape(TERTIARY_POINTS, N_SCEN, UNIT_SAMPLES, sample_patch_pattern.shape[1])
    node_factor, condensed = lax.map(node_work, (grouped, factors_bundled, mask_grouped, terminal_penalty_entries, terminal_ancestor_coupler))
    node_parent = jnp.arange(TERTIARY_POINTS, dtype=jnp.int32) * PARENTS // TERTIARY_POINTS
    owners = (node_parent[None, :] == jnp.arange(PARENTS, dtype=jnp.int32)[:, None]).astype(jnp.float32)
    sums = jnp.einsum('pn,nij->pij', owners, condensed, precision=lax.Precision.HIGHEST)
    parent_block = sums + jax.vmap(jnp.diag)(secondary_penalty_entries)
    parent_factor = jnp.linalg.cholesky(parent_block)
    solve_one = lambda fac, rhs: jax.scipy.linalg.solve_triangular(fac, rhs, lower=True)
    parent_reduced = jax.vmap(solve_one)(parent_factor, secondary_base_coupler.astype(jnp.float32))
    pieces = jnp.einsum('bpr,bps->rs', parent_reduced, parent_reduced, precision=lax.Precision.HIGHEST)
    root_block = jnp.diag(opening_penalty_entries) + pieces
    root_factor = jnp.linalg.cholesky(root_block)
    return (node_factor, parent_factor, root_factor)
```

```python
import jax
import jax.numpy as jnp
from jax import lax
from jax.experimental import pallas as pl
from jax.experimental.pallas import tpu as pltpu
from jax.sharding import Mesh, PartitionSpec as P

F = jnp.float32
HI = lax.Precision.HIGHEST

NEWT=1
def recip(d):
    r=pl.reciprocal(d,approx=True)
    for _ in range(NEWT): r=r*(2.0-d*r)
    return r
def chol_tiles(chains):
    row=lax.broadcasted_iota(jnp.int32,(8,128),0); col=lax.broadcasted_iota(jnp.int32,(8,128),1)
    full=lambda v: jnp.broadcast_to(v,(8,128))
    T=len(chains[0])
    st=[]
    for tiles in chains:
        st.append((list(tiles),[(col==row+8*t).astype(F) for t in range(T)],[],[]))
    for g in range(T):
        for Xa,Xw,U,W in st:
            b0=8*g
            C={t:[full(Xa[t][:,b0+k:b0+k+1]) for k in range(8)] for t in range(g,T)}
            s=[[full(C[g][k][i:i+1,:]) if i>=k else None for k in range(8)] for i in range(8)]
            Ra=[full(Xa[g][i:i+1,:]) for i in range(8)]
            Rw=[full(Xw[g][i:i+1,:]) for i in range(8)]
            upd=[]
            u=w=jnp.zeros((8,128),F)
            for k in range(0,8,2):
                k1=k+1
                a=s[k][k]; b=s[k1][k]; c=s[k1][k1]
                det=a*c-b*b
                rd=recip(det); ra=recip(a)
                ia=c*rd; ib=b*rd; ic=a*rd
                for l in range(k+2,8):
                    p=(c*s[l][k]-b*s[l][k1])*rd; q=(a*s[l][k1]-b*s[l][k])*rd
                    for i in range(l,8): s[i][l]=s[i][l]-(p*s[i][k]+q*s[i][k1])
                    Ra[l]=Ra[l]-(p*Ra[k]+q*Ra[k1]); Rw[l]=Rw[l]-(p*Rw[k]+q*Rw[k1])
                    for t in range(g+1,T): C[t][l]=C[t][l]-(p*C[t][k]+q*C[t][k1])
                upd.append((ia,ib,ic))
                m=b*ra
                q0=lax.rsqrt(a); q1=lax.rsqrt(det*ra)
                u=jnp.where(row==k,Ra[k]*q0,jnp.where(row==k1,(Ra[k1]-m*Ra[k])*q1,u))
                w=jnp.where(row==k,Rw[k]*q0,jnp.where(row==k1,(Rw[k1]-m*Rw[k])*q1,w))
            for t in range(g+1,T):
                for k in range(0,8,2):
                    ia,ib,ic=upd[k//2]
                    x=C[t][k]; y=C[t][k+1]
                    c0=ia*x-ib*y; c1=ic*y-ib*x
                    Xa[t]=Xa[t]-(c0*Ra[k]+c1*Ra[k+1]); Xw[t]=Xw[t]-(c0*Rw[k]+c1*Rw[k+1])
            U.append(jnp.where(col>=row+b0,u,0.0)); W.append(w)
    return [(U,W) for _,_,U,W in st]
OFF=[sum(8-q for q in range(k)) for k in range(9)]
NC=4
def schur_kernel(x_hbm, w_ref, p_ref, s_ref, x_v, half, ht, sq, sem):
    n=x_v.shape[0]; c=n//NC
    cps=[pltpu.make_async_copy(x_hbm.at[pl.ds(q*c,c)],x_v.at[pl.ds(q*c,c)],sem.at[q]) for q in range(NC)]
    for cp in cps: cp.start()
    rw=jnp.sqrt(w_ref[...])
    sq[...]=jnp.concatenate([rw]*8,0).T
    for q in range(NC):
        cps[q].wait()
        for s in range(q*c,(q+1)*c):
            col=jnp.broadcast_to(sq[:,s:s+1],(128,128))
            for j in range(8):
                m=p_ref[s,j].astype(F)
                half[s*128:(s+1)*128,j*128:(j+1)*128]=(x_v[s,:,j*128:(j+1)*128].astype(F)*col*m).astype(jnp.bfloat16)
            for j in range(4):
                ht[j*256:(j+1)*256,s*128:(s+1)*128]=half[s*128:(s+1)*128,j*256:(j+1)*256].T
    for J in range(4):
        for I in range(J,4):
            r=jnp.dot(ht[I*256:(I+1)*256,:],half[:,J*256:(J+1)*256],preferred_element_type=F)
            for a in range(2):
                for b in range(2):
                    i,j=2*I+a,2*J+b
                    if i>=j:
                        o=(OFF[j]+i-j)*128
                        s_ref[o:o+128,:]=r[a*128:(a+1)*128,b*128:(b+1)*128]
def schur(x,w,p):
    n=x.shape[0]
    return pl.pallas_call(schur_kernel,out_shape=jax.ShapeDtypeStruct((36*128,128),F),
      in_specs=[pl.BlockSpec(memory_space=pl.ANY),pl.BlockSpec(memory_space=pltpu.VMEM),pl.BlockSpec(memory_space=pltpu.SMEM)],
      out_specs=pl.BlockSpec(memory_space=pltpu.VMEM),
      scratch_shapes=[pltpu.VMEM((n,128,1024),jnp.bfloat16),pltpu.VMEM((n*128,1024),jnp.bfloat16),pltpu.VMEM((1024,n*128),jnp.bfloat16),pltpu.VMEM((128,128),F),pltpu.SemaphoreType.DMA((NC,))],
      compiler_params=pltpu.CompilerParams(vmem_limit_bytes=40<<20),
      cost_estimate=pl.CostEstimate(flops=1<<32,bytes_accessed=6<<20,transcendentals=2048),
      name="schur_term")(x,w,p)
def dnt(a,b,prec=HI):
    return lax.dot_general(a,b,(((1,),(1,)),((),())),precision=prec,preferred_element_type=F)
NB=8; B=128
OFF=[sum(NB-q for q in range(k)) for k in range(NB+1)]
def chol_vals(ds):
    res=chol_tiles([[d[8*t:8*t+8,:] for t in range(16)] for d in ds])
    return [(jnp.concatenate(U,0).T, jnp.concatenate(W,0)) for U,W in res]
def diag_mat(v):
    r=lax.broadcasted_iota(jnp.int32,(128,128),0); c=lax.broadcasted_iota(jnp.int32,(128,128),1)
    return jnp.where(r==c,jnp.broadcast_to(v,(128,128)),0.0)
def node_kernel(row0_ref, s_ref, diag_ref, ct_ref, own_ref, cond_ref, *panels):
    for k in range(NB):
        n=(NB-k)*B
        panels[k][0:n,:]=s_ref[OFF[k]*B:OFF[k+1]*B,:]
        panels[k][0:B,:]=panels[k][0:B,:]+diag_mat(diag_ref[:,k*B:(k+1)*B])
        panels[k][n:n+256,:]=ct_ref[:,k*B:(k+1)*B]
    for k in range(NB):
        (L,W),=chol_vals([panels[k][0:B,:]])
        n=(NB-k)*B+256
        lp=dnt(panels[k][B:n,:],W)
        panels[k][0:B,:]=L
        panels[k][B:n,:]=lp
        for j in range(k+1,NB):
            o=(j-k)*B
            panels[j][...]=panels[j][...]-dnt(panels[k][o:n,:],panels[k][o:o+B,:])
    acc=None
    for k in range(NB):
        n=(NB-k)*B
        c=panels[k][n:n+256,:]
        t=dnt(c,c)
        acc=t if acc is None else acc+t
    cond_ref[...]=acc
    r0=row0_ref[0]
    b=r0//B; off=r0-b*B
    own_ref[...]=jnp.zeros(own_ref.shape,F)
    for k in range(NB):
        @pl.when(b>=k)
        def _():
            own_ref[:,k*B:(k+1)*B]=panels[k][pl.ds(pl.multiple_of((b-k)*B+off,16),16),:]
def node_factor(row0, s, diag, ct):
    return pl.pallas_call(node_kernel,
      out_shape=[jax.ShapeDtypeStruct((16,1024),F),jax.ShapeDtypeStruct((256,256),F)],
      in_specs=[pl.BlockSpec(memory_space=pltpu.SMEM)]+[pl.BlockSpec(memory_space=pltpu.VMEM)]*3,
      out_specs=[pl.BlockSpec(memory_space=pltpu.VMEM)]*2,
      scratch_shapes=[pltpu.VMEM(((10-k)*B,B),F) for k in range(NB)],
      compiler_params=pltpu.CompilerParams(vmem_limit_bytes=40<<20),
      cost_estimate=pl.CostEstimate(flops=1<<32,bytes_accessed=8<<20,transcendentals=1<<14),
      name="node_factor")(row0,s,diag,ct)
def tail_kernel(s_ref, diag_ref, bt_ref, od_ref, pf_ref, rf_ref):
    d0=[s_ref[p,0:B,:]+diag_mat(diag_ref[p:p+1,0:B]) for p in range(2)]
    r0=chol_vals(d0)
    d1=[];lb0=[];l10=[]
    for p in range(2):
        L,W=r0[p]
        l10.append(dnt(s_ref[p,B:2*B,:],W)); lb0.append(dnt(bt_ref[p,:,0:B],W))
        d1.append(s_ref[p,2*B:,:]+diag_mat(diag_ref[p:p+1,B:])-dnt(l10[p],l10[p]))
        pf_ref[p,0:B,0:B]=L; pf_ref[p,0:B,B:]=jnp.zeros((B,B),F); pf_ref[p,B:,0:B]=l10[p]
    r1=chol_vals(d1)
    root=diag_mat(od_ref[...])
    for p in range(2):
        L,W=r1[p]
        pf_ref[p,B:,B:]=L
        lb1=dnt(bt_ref[p,:,B:]-dnt(lb0[p],l10[p]),W)
        root=root+dnt(lb0[p],lb0[p])+dnt(lb1,lb1)
    (L,_),=chol_vals([root])
    rf_ref[...]=L
def tail(s,diag,bt,od):
    return pl.pallas_call(tail_kernel,
      out_shape=[jax.ShapeDtypeStruct((2,256,256),F),jax.ShapeDtypeStruct((128,128),F)],
      in_specs=[pl.BlockSpec(memory_space=pltpu.VMEM)]*4,
      out_specs=[pl.BlockSpec(memory_space=pltpu.VMEM)]*2,
      compiler_params=pltpu.CompilerParams(vmem_limit_bytes=40<<20),
      name="tail")(s,diag,bt,od)
def per_device(samples, weights, pattern, diag, coupler, diag2, coupler2, diag3):
    s = schur(samples, weights, pattern)
    s = lax.all_to_all(s, "x", 0, 0, tiled=True).reshape(4, 1152, 128).sum(0)
    s = lax.all_to_all(s, "z", 0, 0, tiled=True).reshape(16, 72, 128).sum(0)
    s = jnp.broadcast_to(s[None], (16, 72, 128)).reshape(1152, 128)
    s = lax.all_to_all(s, "z", 0, 0, tiled=True)
    s = jnp.broadcast_to(s[None], (4, 1152, 128)).reshape(4608, 128)
    s = lax.all_to_all(s, "x", 0, 0, tiled=True)
    row0 = (lax.axis_index("z") * 4 + lax.axis_index("x")) * 16
    own, cond = node_factor(row0.reshape(1).astype(jnp.int32), s, diag, coupler[0].astype(F).T)
    low = jnp.concatenate([cond[:128, :128], cond[128:, :128], cond[128:, 128:]], 0)
    low = low + lax.ppermute(low, "core", [(0, 1), (1, 0)])
    low = lax.all_gather(low, "y", axis=0)
    low = low.reshape(2, 2, 384, 128).sum(1)
    parent, root = tail(low, diag2, jnp.swapaxes(coupler2.astype(F), 1, 2), diag3[None])
    return own[None], parent, root


def solution(mesh):
    sizes = mesh.devices.shape
    devices = mesh.devices.reshape(4, 2, 16, 4)
    split = Mesh(devices, ("y", "core", "z", "x"))
    node, scen = ("y", "core"), ("z", "x")
    return jax.shard_map(
        per_device,
        mesh=split,
        in_specs=(P(node + scen, None, None), P(node + scen, None), P(node + scen, None), P(node, None), P(node, None, None), P(), P(), P()),
        out_specs=(P(node, scen, None), P(), P()),
        check_vma=False,
    )
```

```python
import jax
import jax.numpy as jnp
from jax import lax
from jax.experimental import pallas as pl
from jax.experimental.pallas import tpu as pltpu
from jax.sharding import Mesh, PartitionSpec as P

F = jnp.float32
HI = lax.Precision.HIGHEST


def dnt(a, b):
    return lax.dot_general(a, b, (((1,), (1,)), ((), ())), precision=HI, preferred_element_type=F)


def dnn(a, b):
    return jnp.dot(a, b, precision=HI, preferred_element_type=F)


def spread(v):
    return jnp.broadcast_to(v, (8, 128))


def lane(v, i):
    return jnp.take_along_axis(v, jnp.full((8, 128), i, jnp.int32), axis=1)


def tree(d):
    return ((d[0] + d[1]) + (d[2] + d[3])) + ((d[4] + d[5]) + (d[6] + d[7]))


def eliminate(halves, count):
    row = lax.broadcasted_iota(jnp.int32, (8, 128), 0)
    X = halves[0]
    out = [[] for _ in halves]
    for g in range(count):
        b0 = 8 * g
        C = {t: [lane(X[t], b0 + k) for k in range(8)] for t in range(g, count)}
        s = [[spread(C[g][k][i : i + 1, :]) if i >= k else None for k in range(8)] for i in range(8)]
        rows = [[spread(H[g][i : i + 1, :]) for i in range(8)] for H in halves]
        res = [jnp.zeros((8, 128), F) for _ in halves]
        steps = []
        for k in range(0, 8, 2):
            k1 = k + 1
            a, b, c = s[k][k], s[k1][k], s[k1][k1]
            det = a * c - b * b
            rd = pl.reciprocal(det, approx=True)
            ra = pl.reciprocal(a, approx=True)
            rd = rd * (2.0 - det * rd)
            ra = ra * (2.0 - a * ra)
            after = range(k + 2, 8)
            pn = {l: c * s[l][k] - b * s[l][k1] for l in after}
            qn = {l: a * s[l][k1] - b * s[l][k] for l in after}
            for l in after:
                for i in range(l, 8):
                    s[i][l] = s[i][l] - rd * (pn[l] * s[i][k] + qn[l] * s[i][k1])
            p = {l: pn[l] * rd for l in after}
            q = {l: qn[l] * rd for l in after}
            steps.append((c * rd, b * rd, a * rd, p, q))
            q0 = lax.rsqrt(a)
            q1 = lax.rsqrt(det * ra)
            m = b * ra
            for h, R in enumerate(rows):
                for l in after:
                    R[l] = R[l] - (p[l] * R[k] + q[l] * R[k1])
                res[h] = jnp.where(row == k, R[k] * q0, jnp.where(row == k1, (R[k1] - m * R[k]) * q1, res[h]))
        for h in range(len(halves)):
            out[h].append(res[h])
        if g + 1 < count:
            for H, R in zip(halves, rows):
                Z = [None] * 8
                for k in range(6, -1, -2):
                    ia, ib, ic, p, q = steps[k // 2]
                    z0 = ia * R[k] - ib * R[k + 1]
                    z1 = ic * R[k + 1] - ib * R[k]
                    for l in range(k + 2, 8, 2):
                        z0 = z0 - (p[l] * Z[l] + p[l + 1] * Z[l + 1])
                        z1 = z1 - (q[l] * Z[l] + q[l + 1] * Z[l + 1])
                    Z[k], Z[k + 1] = z0, z1
                for t in range(g + 1, count):
                    H[t] = H[t] - tree([C[t][k] * Z[k] for k in range(8)])
        yield
    return [jnp.concatenate(o, 0) for o in out]


def lower_of(u):
    n = u.shape[0]
    keep = lax.broadcasted_iota(jnp.int32, (n, n), 1) >= lax.broadcasted_iota(jnp.int32, (n, n), 0)
    return jnp.where(keep, u, 0.0).T


def chol128(D):
    row = lax.broadcasted_iota(jnp.int32, (8, 128), 0)
    col = lax.broadcasted_iota(jnp.int32, (8, 128), 1)
    X = [D[8 * t : 8 * t + 8, :] for t in range(16)]
    Y = [(col == row + 8 * t).astype(F) for t in range(16)]
    U, W = yield from eliminate([X, Y], 16)
    return lower_of(U), W


def chol64(A):
    eye = lax.broadcasted_iota(jnp.int32, (64, 64), 0) == lax.broadcasted_iota(jnp.int32, (64, 64), 1)
    both = jnp.concatenate([A, eye.astype(F)], 1)
    (UW,) = yield from eliminate([[both[8 * t : 8 * t + 8, :] for t in range(8)]], 8)
    return lower_of(UW[:, 0:64]), UW[:, 64:128]


def chol128_halves(D):
    L1, W1 = yield from chol64(D[0:64, 0:64])
    L21 = dnt(D[64:, 0:64], W1)
    L2, W2 = yield from chol64(D[64:, 64:] - dnt(L21, L21))
    W21 = -dnn(W2, dnn(L21, W1))
    z = jnp.zeros((64, 64), F)
    L = jnp.concatenate([jnp.concatenate([L1, z], 1), jnp.concatenate([L21, L2], 1)], 0)
    W = jnp.concatenate([jnp.concatenate([W1, z], 1), jnp.concatenate([W21, W2], 1)], 0)
    return L, W


def run(gens, jobs=()):
    jobs = list(jobs)
    res, live, left = [None] * len(gens), list(range(len(gens))), 14
    while live:
        for i in list(live):
            try:
                next(gens[i])
            except StopIteration as e:
                res[i] = e.value
                live.remove(i)
        for _ in range(-(-len(jobs) // max(left, 1))):
            jobs.pop(0)()
        left -= 1
    for job in jobs:
        job()
    return res
B = 128
NB = 8
OFF = [sum(NB - q for q in range(k)) * B for k in range(NB + 1)]
PIECES = 4


def schur_kernel(x_hbm, w_hbm, p_hbm, s_ref, x, w, p, half, turned, roots, sems):
    size = x.shape[0] // PIECES
    small = [pltpu.make_async_copy(w_hbm, w, sems.at[PIECES]), pltpu.make_async_copy(p_hbm, p, sems.at[PIECES + 1])]
    pieces = [pltpu.make_async_copy(x_hbm.at[pl.ds(q * size, size)], x.at[pl.ds(q * size, size)], sems.at[q]) for q in range(PIECES)]
    for copy in small + pieces:
        copy.start()
    for copy in small:
        copy.wait()
    roots[...] = jnp.concatenate([jnp.sqrt(w[...])] * 8, 0).T
    for q in range(PIECES):
        pieces[q].wait()
        for s in range(q * size, (q + 1) * size):
            here = slice(s * B, (s + 1) * B)
            col = jnp.broadcast_to(roots[:, s : s + 1], (B, B))
            for j in range(NB):
                mask = p[j, s].astype(F)
                half[here, j * B : (j + 1) * B] = (x[s, :, j * B : (j + 1) * B].astype(F) * col * mask).astype(jnp.bfloat16)
            for j in range(4):
                turned[j * 256 : (j + 1) * 256, here] = half[here, j * 256 : (j + 1) * 256].T
        if q % 2 == 1:
            rows = slice((q - 1) * size * B, (q + 1) * size * B)
            for J in range(4):
                for I in range(J, 4):
                    r = jnp.dot(turned[I * 256 : (I + 1) * 256, rows], half[rows, J * 256 : (J + 1) * 256], preferred_element_type=F)
                    for a in range(2):
                        for b in range(2):
                            i, j = 2 * I + a, 2 * J + b
                            if i >= j:
                                o = OFF[j] + (i - j) * B
                                t = r[a * B : (a + 1) * B, b * B : (b + 1) * B]
                                s_ref[o : o + B, :] = t if q == 1 else s_ref[o : o + B, :] + t


def schur(x, w, p):
    n = x.shape[0]
    return pl.pallas_call(
        schur_kernel,
        out_shape=jax.ShapeDtypeStruct((36 * B, B), F),
        in_specs=[pl.BlockSpec(memory_space=pl.ANY)] * 3,
        out_specs=pl.BlockSpec(memory_space=pltpu.VMEM),
        scratch_shapes=[
            pltpu.VMEM((n, B, NB * B), jnp.bfloat16),
            pltpu.VMEM((n, B), F),
            pltpu.SMEM((NB, n), jnp.int32),
            pltpu.VMEM((n * B, NB * B), jnp.bfloat16),
            pltpu.VMEM((NB * B, n * B), jnp.bfloat16),
            pltpu.VMEM((B, B), F),
            pltpu.SemaphoreType.DMA((PIECES + 2,)),
        ],
        compiler_params=pltpu.CompilerParams(vmem_limit_bytes=58 << 20),
        cost_estimate=pl.CostEstimate(flops=1 << 32, bytes_accessed=6 << 20, transcendentals=2048),
        name="schur_term",
    )(x, w, p.T)
VM = pl.BlockSpec(memory_space=pltpu.VMEM)


def diag_mat(v):
    r = lax.broadcasted_iota(jnp.int32, (B, B), 0)
    c = lax.broadcasted_iota(jnp.int32, (B, B), 1)
    return jnp.where(r == c, jnp.broadcast_to(v, (B, B)), 0.0)


def panel_rows(k):
    return (NB - k) * B + 256


def node_kernel(row0_ref, s_ref, diag_ref, c_ref, own_ref, cond, *panels):
    def base(j, lo, hi):
        n = (NB - j) * B
        parts = []
        if lo == 0:
            parts.append(block(j))
        if max(lo, B) < min(hi, n):
            parts.append(s_ref[OFF[j] + max(lo, B) : OFF[j] + min(hi, n), :])
        if hi > n:
            parts.append(c_ref[0, j * B : (j + 1) * B, max(lo - n, 0) : hi - n].astype(F).T)
        return parts[0] if len(parts) == 1 else jnp.concatenate(parts, 0)

    def block(j):
        return s_ref[OFF[j] : OFF[j] + B, :] + diag_mat(diag_ref[:, j * B : (j + 1) * B])

    def solve(k, W, lo, hi):
        def job():
            panels[k][lo:hi, :] = dnt(base(k, lo, hi) if k == 0 else panels[k][lo:hi, :], W)
        return job

    def update(j, lo, hi, ks):
        def job():
            left = [panels[k][(j - k) * B + lo : (j - k) * B + hi, :] for k in ks]
            right = [panels[k][(j - k) * B : (j - k) * B + B, :] for k in ks]
            both = [v[0] if len(ks) == 1 else jnp.concatenate(v, 1) for v in (left, right)]
            panels[j][lo:hi, :] = (base(j, lo, hi) if ks[0] == 0 else panels[j][lo:hi, :]) - dnt(*both)
        return job

    def gather(ks, lo):
        def job():
            c = jnp.concatenate([panels[k][panel_rows(k) - 256 :, :] for k in ks], 1)
            t = dnt(c[lo : lo + B, :], c)
            cond[lo : lo + B, :] = t if ks[0] == 0 else cond[lo : lo + B, :] + t
        return job

    def cut(lo, hi):
        return [(a, min(a + 256, hi)) for a in range(lo, hi, 256)]

    D = block(0)
    jobs = []
    for k in range(NB):
        ((L, W),) = run([chol128(D)], jobs)
        n = panel_rows(k)
        panels[k][0:B, :] = L
        jobs = []
        start = B
        if k + 1 < NB:
            solve(k, W, B, 2 * B)()
            top = panels[k][B : 2 * B, :]
            start = 2 * B
            if k % 2 == 0:
                D = (block(k + 1) if k == 0 else panels[k + 1][0:B, :]) - dnt(top, top)
            else:
                two = jnp.concatenate([panels[k - 1][2 * B : 3 * B, :], top], 1)
                D = (block(k + 1) if k == 1 else panels[k + 1][0:B, :]) - dnt(two, two)
        jobs += [solve(k, W, lo, hi) for lo, hi in cut(start, n)]
        if k + 1 < NB:
            if k % 2 == 0:
                jobs += [update(k + 1, lo, hi, [k]) for lo, hi in cut(B, panel_rows(k + 1))]
            else:
                for j in range(k + 1, NB):
                    jobs += [update(j, lo, hi, [k - 1, k]) for lo, hi in cut(B if j == k + 1 else 0, panel_rows(j))]
        if k % 2 == 1:
            jobs += [gather([k - 1, k], 0), gather([k - 1, k], B)]
    for job in jobs:
        job()
    r0 = row0_ref[0]
    b = r0 // B
    off = r0 - b * B
    own_ref[...] = jnp.zeros(own_ref.shape, F)
    for k, panel in enumerate(panels):
        @pl.when(b >= k)
        def _():
            own_ref[:, k * B : (k + 1) * B] = panel[pl.ds(pl.multiple_of((b - k) * B + off, 16), 16), :]


def node_factor(row0, s, diag, coupler):
    return pl.pallas_call(
        node_kernel,
        out_shape=[jax.ShapeDtypeStruct((16, 1024), F), jax.ShapeDtypeStruct((256, 256), F)],
        in_specs=[pl.BlockSpec(memory_space=pltpu.SMEM)] + [VM] * 3,
        out_specs=[VM] * 2,
        scratch_shapes=[pltpu.VMEM((panel_rows(k), B), F) for k in range(NB)],
        compiler_params=pltpu.CompilerParams(vmem_limit_bytes=24 << 20),
        cost_estimate=pl.CostEstimate(flops=1 << 33, bytes_accessed=8 << 20, transcendentals=1 << 14),
        name="node_factor",
    )(row0, s, diag, coupler)


def tail_kernel(s_ref, diag_ref, c_ref, od_ref, pf_ref, rf_ref):
    d0 = [s_ref[p, 0:B, :] + diag_mat(diag_ref[p : p + 1, 0:B]) for p in range(2)]
    r0 = run([chol128_halves(d) for d in d0])
    l10, lb0, d1, parts = [], [], [], []
    for p in range(2):
        L, W = r0[p]
        l10.append(dnt(s_ref[p, B : 2 * B, :], W))
        d1.append(s_ref[p, 2 * B :, :] + diag_mat(diag_ref[p : p + 1, B:]) - dnt(l10[p], l10[p]))
        pf_ref[p, 0:B, 0:B] = L
        pf_ref[p, 0:B, B:] = jnp.zeros((B, B), F)
        pf_ref[p, B:, 0:B] = l10[p]

    def early(p):
        def job():
            lb0.append(dnt(c_ref[p, 0:B, :].astype(F).T, r0[p][1]))
            parts.append((c_ref[p, B:, :].astype(F).T - dnt(lb0[p], l10[p]), dnt(lb0[p], lb0[p])))
        return job

    r1 = run([chol128_halves(d) for d in d1], [early(0), early(1)])
    root = diag_mat(od_ref[...])
    for p in range(2):
        L, W = r1[p]
        pf_ref[p, B:, B:] = L
        lb1 = dnt(parts[p][0], W)
        root = root + parts[p][1] + dnt(lb1, lb1)
    ((L, _),) = run([chol128(root)])
    rf_ref[...] = L


def tail(s, diag, coupler, od):
    return pl.pallas_call(
        tail_kernel,
        out_shape=[jax.ShapeDtypeStruct((2, 256, 256), F), jax.ShapeDtypeStruct((128, 128), F)],
        in_specs=[VM] * 4,
        out_specs=[VM] * 2,
        compiler_params=pltpu.CompilerParams(vmem_limit_bytes=24 << 20),
        cost_estimate=pl.CostEstimate(flops=1 << 30, bytes_accessed=2 << 20, transcendentals=1 << 14),
        name="tail",
    )(s, diag, coupler, od)
def split(r, parts):
    return r.reshape(parts, r.shape[0] // parts, 128)


def added(r, axis, parts):
    return split(lax.all_to_all(r, axis, 0, 0, tiled=True), parts).sum(0)


def everywhere(r, axis, parts):
    copies = jnp.broadcast_to(r[None], (parts,) + r.shape).reshape(parts * r.shape[0], 128)
    return lax.all_to_all(copies, axis, 0, 0, tiled=True)


def per_device(samples, weights, pattern, diag, coupler, diag2, coupler2, diag3):
    s = schur(samples, weights, pattern)
    s = added(s, "x", 4)
    s = added(s, "zl", 4)
    s = split(lax.all_gather(s, "zh", axis=0, tiled=True), 4).sum(0)
    s = lax.all_gather(s, "zl", axis=0, tiled=True)
    row0 = ((lax.axis_index(("zh", "zl")) * 4 + lax.axis_index("x")) * 16).reshape(1).astype(jnp.int32)
    s, row0 = lax.optimization_barrier((s, row0))
    s = everywhere(s, "x", 4)
    own, cond = node_factor(row0, s, diag, coupler)
    low = jnp.concatenate([cond[:B, :B], cond[B:, :B], cond[B:, B:]], 0)
    low = low + lax.ppermute(low, "core", [(0, 1), (1, 0)])
    low = lax.all_gather(low, "y", axis=0).reshape(2, 2, 3 * B, B).sum(1)
    parent, root = tail(low, diag2, coupler2, diag3[None])
    return own[None], parent, root


def solution(mesh):
    devices = mesh.devices.reshape(4, 2, 4, 4, 4)
    finer = Mesh(devices, ("y", "core", "zh", "zl", "x"))
    node, scen = ("y", "core"), ("zh", "zl", "x")
    return jax.shard_map(
        per_device,
        mesh=finer,
        in_specs=(P(node + scen, None, None), P(node + scen, None), P(node + scen, None), P(node, None), P(node, None, None), P(), P(), P()),
        out_specs=(P(node, scen, None), P(), P()),
        check_vma=False,
    )
```

```python
import jax
import jax.numpy as jnp
from jax import lax
from jax.experimental import pallas as pl
from jax.experimental.pallas import tpu as pltpu
from jax.sharding import Mesh, PartitionSpec as P

F = jnp.float32
HI = lax.Precision.HIGHEST


def dnt(a, b):
    return lax.dot_general(a, b, (((1,), (1,)), ((), ())), precision=HI, preferred_element_type=F)


def dnn(a, b):
    return jnp.dot(a, b, precision=HI, preferred_element_type=F)


def spread(v):
    return jnp.broadcast_to(v, (8, 128))


def lane(v, i):
    return jnp.take_along_axis(v, jnp.full((8, 128), i, jnp.int32), axis=1)


def tree(d):
    return ((d[0] + d[1]) + (d[2] + d[3])) + ((d[4] + d[5]) + (d[6] + d[7]))


def eliminate(X):
    row = lax.broadcasted_iota(jnp.int32, (8, 128), 0)
    col = lax.broadcasted_iota(jnp.int32, (8, 128), 1)
    X = list(X)
    count = len(X)
    out = [[], []]
    for g in range(count):
        b0 = 8 * g
        C = {t: [lane(X[t], b0 + k) for k in range(8)] for t in range(g, count)}
        s = [[spread(C[g][k][i : i + 1, :]) if i >= k else None for k in range(8)] for i in range(8)]
        upper = [spread(X[g][i : i + 1, :]) for i in range(8)]
        inverse = [jnp.where(col < b0, upper[i], jnp.where(col == b0 + i, 1.0, 0.0)) for i in range(8)]
        rows = [upper, inverse]
        res = [jnp.zeros((8, 128), F) for _ in rows]
        steps = []
        for k in range(0, 8, 2):
            k1 = k + 1
            a, b, c = s[k][k], s[k1][k], s[k1][k1]
            det = a * c - b * b
            rd = pl.reciprocal(det, approx=True)
            ra = pl.reciprocal(a, approx=True)
            after = range(k + 2, 8)
            pn = {l: c * s[l][k] - b * s[l][k1] for l in after}
            qn = {l: a * s[l][k1] - b * s[l][k] for l in after}
            for l in after:
                for i in range(l, 8):
                    s[i][l] = s[i][l] - rd * (pn[l] * s[i][k] + qn[l] * s[i][k1])
            p = {l: pn[l] * rd for l in after}
            q = {l: qn[l] * rd for l in after}
            steps.append((c * rd, b * rd, a * rd, p, q))
            q0 = lax.rsqrt(a)
            q1 = lax.rsqrt(det * ra)
            m = b * ra
            for h, R in enumerate(rows):
                for l in after:
                    R[l] = R[l] - (p[l] * R[k] + q[l] * R[k1])
                res[h] = jnp.where(row == k, R[k] * q0, jnp.where(row == k1, (R[k1] - m * R[k]) * q1, res[h]))
        for o, v in zip(out, res):
            o.append(v)
        if g + 1 < count:
            V = [jnp.where(col < b0 + 8, inverse[k], upper[k]) for k in range(8)]
            Z = [None] * 8
            for k in range(6, -1, -2):
                ia, ib, ic, p, q = steps[k // 2]
                z0 = ia * V[k] - ib * V[k + 1]
                z1 = ic * V[k + 1] - ib * V[k]
                for l in range(k + 2, 8, 2):
                    z0 = z0 - (p[l] * Z[l] + p[l + 1] * Z[l + 1])
                    z1 = z1 - (q[l] * Z[l] + q[l + 1] * Z[l + 1])
                Z[k], Z[k + 1] = z0, z1
            pivots = (col >= b0) & (col < b0 + 8)
            for t in range(g + 1, count):
                X[t] = jnp.where(pivots, 0.0, X[t]) - tree([C[t][k] * Z[k] for k in range(8)])
        yield
    return [jnp.concatenate(o, 0) for o in out]


def eliminate_beside(halves, count):
    row = lax.broadcasted_iota(jnp.int32, (8, 128), 0)
    X = halves[0]
    out = [[] for _ in halves]
    for g in range(count):
        b0 = 8 * g
        C = {t: [lane(X[t], b0 + k) for k in range(8)] for t in range(g, count)}
        s = [[spread(C[g][k][i : i + 1, :]) if i >= k else None for k in range(8)] for i in range(8)]
        rows = [[spread(H[g][i : i + 1, :]) for i in range(8)] for H in halves]
        res = [jnp.zeros((8, 128), F) for _ in halves]
        steps = []
        for k in range(0, 8, 2):
            k1 = k + 1
            a, b, c = s[k][k], s[k1][k], s[k1][k1]
            det = a * c - b * b
            rd = pl.reciprocal(det, approx=True)
            ra = pl.reciprocal(a, approx=True)
            after = range(k + 2, 8)
            pn = {l: c * s[l][k] - b * s[l][k1] for l in after}
            qn = {l: a * s[l][k1] - b * s[l][k] for l in after}
            for l in after:
                for i in range(l, 8):
                    s[i][l] = s[i][l] - rd * (pn[l] * s[i][k] + qn[l] * s[i][k1])
            p = {l: pn[l] * rd for l in after}
            q = {l: qn[l] * rd for l in after}
            steps.append((c * rd, b * rd, a * rd, p, q))
            q0 = lax.rsqrt(a)
            q1 = lax.rsqrt(det * ra)
            m = b * ra
            for h, R in enumerate(rows):
                for l in after:
                    R[l] = R[l] - (p[l] * R[k] + q[l] * R[k1])
                res[h] = jnp.where(row == k, R[k] * q0, jnp.where(row == k1, (R[k1] - m * R[k]) * q1, res[h]))
        for h in range(len(halves)):
            out[h].append(res[h])
        if g + 1 < count:
            for H, R in zip(halves, rows):
                Z = [None] * 8
                for k in range(6, -1, -2):
                    ia, ib, ic, p, q = steps[k // 2]
                    z0 = ia * R[k] - ib * R[k + 1]
                    z1 = ic * R[k + 1] - ib * R[k]
                    for l in range(k + 2, 8, 2):
                        z0 = z0 - (p[l] * Z[l] + p[l + 1] * Z[l + 1])
                        z1 = z1 - (q[l] * Z[l] + q[l + 1] * Z[l + 1])
                    Z[k], Z[k + 1] = z0, z1
                for t in range(g + 1, count):
                    H[t] = H[t] - tree([C[t][k] * Z[k] for k in range(8)])
        yield
    return [jnp.concatenate(o, 0) for o in out]


def lower_of(u):
    n = u.shape[0]
    keep = lax.broadcasted_iota(jnp.int32, (n, n), 1) >= lax.broadcasted_iota(jnp.int32, (n, n), 0)
    return jnp.where(keep, u, 0.0).T


def chol128(D):
    U, W = yield from eliminate([D[8 * t : 8 * t + 8, :] for t in range(16)])
    return lower_of(U), W


def chol64(A):
    eye = lax.broadcasted_iota(jnp.int32, (64, 64), 0) == lax.broadcasted_iota(jnp.int32, (64, 64), 1)
    both = jnp.concatenate([A, eye.astype(F)], 1)
    (UW,) = yield from eliminate_beside([[both[8 * t : 8 * t + 8, :] for t in range(8)]], 8)
    return lower_of(UW[:, 0:64]), UW[:, 64:128]


def chol128_halves(D):
    L1, W1 = yield from chol64(D[0:64, 0:64])
    L21 = dnt(D[64:, 0:64], W1)
    L2, W2 = yield from chol64(D[64:, 64:] - dnt(L21, L21))
    W21 = -dnn(W2, dnn(L21, W1))
    z = jnp.zeros((64, 64), F)
    L = jnp.concatenate([jnp.concatenate([L1, z], 1), jnp.concatenate([L21, L2], 1)], 0)
    W = jnp.concatenate([jnp.concatenate([W1, z], 1), jnp.concatenate([W21, W2], 1)], 0)
    return L, W


def run(gens, jobs=()):
    jobs = list(jobs)
    res, live, left = [None] * len(gens), list(range(len(gens))), 14
    while live:
        for i in list(live):
            try:
                next(gens[i])
            except StopIteration as e:
                res[i] = e.value
                live.remove(i)
        for _ in range(-(-len(jobs) // max(left, 1))):
            jobs.pop(0)()
        left -= 1
    for job in jobs:
        job()
    return res
B = 128
NB = 8
OFF = [sum(NB - 1 - q for q in range(k)) * B for k in range(NB + 1)]
DIAG = OFF[NB]
CORNER = DIAG + NB * 64
ROWS = CORNER + NB * 32
PIECES = 4


def schur_kernel(x_hbm, w_hbm, p_hbm, s_ref, x, w, p, half, roots, sems):
    size = x.shape[0] // PIECES
    small = [pltpu.make_async_copy(w_hbm, w, sems.at[PIECES]), pltpu.make_async_copy(p_hbm, p, sems.at[PIECES + 1])]
    pieces = [pltpu.make_async_copy(x_hbm.at[pl.ds(q * size, size)], x.at[pl.ds(q * size, size)], sems.at[q]) for q in range(PIECES)]
    for copy in small + pieces:
        copy.start()
    for copy in small:
        copy.wait()
    roots[...] = jnp.concatenate([jnp.sqrt(w[...])] * 8, 0).T
    first = lax.broadcasted_iota(jnp.int32, (64, B), 1) < 64
    for q in range(PIECES):
        pieces[q].wait()
        for s in range(q * size, (q + 1) * size):
            here = slice(s * B, (s + 1) * B)
            col = jnp.broadcast_to(roots[:, s : s + 1], (B, B))
            for j in range(NB):
                mask = p[j, s].astype(F).astype(jnp.bfloat16)
                half[here, j * B : (j + 1) * B] = (x[s, :, j * B : (j + 1) * B].astype(F) * col).astype(jnp.bfloat16) * mask
        if q % 2 == 1:
            rows = slice((q - 1) * size * B, (q + 1) * size * B)
            for J in range(4):
                for I in range(J, 4):
                    r = lax.dot_general(half[rows, I * 256 : (I + 1) * 256], half[rows, J * 256 : (J + 1) * 256], (((0,), (0,)), ((), ())), preferred_element_type=F)
                    whole = {(2 * I + a, 2 * J + b): r[a * B : (a + 1) * B, b * B : (b + 1) * B] for a in range(2) for b in range(2)}
                    out = [(OFF[j] + (i - j - 1) * B, t) for (i, j), t in whole.items() if i > j]
                    if I == J:
                        even, odd = whole[2 * I, 2 * I], whole[2 * I + 1, 2 * I + 1]
                        out.append((DIAG + 2 * I * 64, jnp.where(first, even[:64], even[64:])))
                        out.append((DIAG + (2 * I + 1) * 64, jnp.where(first, odd[:64], odd[64:])))
                        out.append((CORNER + I * 64, jnp.where(first, even[64:], odd[:64])))
                    for o, t in out:
                        here = slice(o, o + t.shape[0])
                        s_ref[here, :] = t if q == 1 else s_ref[here, :] + t


def schur(x, w, p):
    n = x.shape[0]
    return pl.pallas_call(
        schur_kernel,
        out_shape=jax.ShapeDtypeStruct((ROWS, B), F),
        in_specs=[pl.BlockSpec(memory_space=pl.ANY)] * 3,
        out_specs=pl.BlockSpec(memory_space=pltpu.VMEM),
        scratch_shapes=[
            pltpu.VMEM((n, B, NB * B), jnp.bfloat16),
            pltpu.VMEM((n, B), F),
            pltpu.SMEM((NB, n), jnp.int32),
            pltpu.VMEM((n * B, NB * B), jnp.bfloat16),
            pltpu.VMEM((B, B), F),
            pltpu.SemaphoreType.DMA((PIECES + 2,)),
        ],
        compiler_params=pltpu.CompilerParams(vmem_limit_bytes=58 << 20),
        cost_estimate=pl.CostEstimate(flops=1 << 32, bytes_accessed=6 << 20, transcendentals=2048),
        name="schur_term",
    )(x, w, p.T)
VM = pl.BlockSpec(memory_space=pltpu.VMEM)


def diag_mat(v):
    r = lax.broadcasted_iota(jnp.int32, (B, B), 0)
    c = lax.broadcasted_iota(jnp.int32, (B, B), 1)
    return jnp.where(r == c, jnp.broadcast_to(v, (B, B)), 0.0)


def panel_rows(k):
    return (NB - k) * B + 256


def cut3(v):
    h = v.astype(jnp.bfloat16)
    r = v - h.astype(F)
    m = r.astype(jnp.bfloat16)
    l = (r - m.astype(F)).astype(jnp.bfloat16)
    return jnp.concatenate([h, m, l], 1)


def times3(pairs):
    left, right = [], []
    for a, b in pairs:
        ah, am, al = (a[:, q * B : (q + 1) * B] for q in range(3))
        bh, bm, bl = (b[:, q * B : (q + 1) * B] for q in range(3))
        left += [ah, ah, am, ah, am, al]
        right += [bh, bm, bh, bl, bm, bh]
    return lax.dot_general(jnp.concatenate(left, 1), jnp.concatenate(right, 1), (((1,), (1,)), ((), ())), preferred_element_type=F)


def node_kernel(row0_ref, s_ref, diag_ref, c_ref, own_ref, cond, *scratch):
    panels, cuts = scratch[:NB], scratch[NB:]

    def block(j):
        here = s_ref[DIAG + j * 64 : DIAG + (j + 1) * 64, :]
        corner = s_ref[CORNER + j // 2 * 64 : CORNER + (j // 2 + 1) * 64, :]
        turned = corner.T
        if j % 2 == 0:
            top = jnp.concatenate([here[:, :64], turned[:64, :]], 1)
            bottom = jnp.concatenate([corner[:, :64], here[:, 64:]], 1)
        else:
            top = jnp.concatenate([here[:, :64], corner[:, 64:]], 1)
            bottom = jnp.concatenate([turned[64:, :], here[:, 64:]], 1)
        return jnp.concatenate([top, bottom], 0) + diag_mat(diag_ref[:, j * B : (j + 1) * B])

    def base(j, lo, hi):
        n = (NB - j) * B
        parts = []
        if lo == 0:
            parts.append(block(j))
        if max(lo, B) < min(hi, n):
            parts.append(s_ref[OFF[j] + max(lo, B) - B : OFF[j] + min(hi, n) - B, :])
        if hi > n:
            parts.append(c_ref[0, j * B : (j + 1) * B, max(lo - n, 0) : hi - n].astype(F).T)
        return parts[0] if len(parts) == 1 else jnp.concatenate(parts, 0)

    def solve(k, W3, lo, hi):
        def job():
            v = times3([(cut3(base(k, lo, hi) if k == 0 else panels[k][lo:hi, :]), W3)])
            panels[k][lo:hi, :] = v
            cuts[k][lo:hi, :] = cut3(v)
        return job

    def update(j, lo, hi, ks):
        def job():
            pairs = [(cuts[k][(j - k) * B + lo : (j - k) * B + hi, :], cuts[k][(j - k) * B : (j - k) * B + B, :]) for k in ks]
            panels[j][lo:hi, :] = (base(j, lo, hi) if ks[0] == 0 else panels[j][lo:hi, :]) - times3(pairs)
        return job

    def gather(ks, lo):
        def job():
            low = [panel_rows(k) - 256 for k in ks]
            t = times3([(cuts[k][o + lo : o + lo + B, :], cuts[k][o:, :]) for k, o in zip(ks, low)])
            cond[lo : lo + B, :] = t if ks[0] == 0 else cond[lo : lo + B, :] + t
        return job

    def spans(lo, hi):
        return [(a, min(a + 256, hi)) for a in range(lo, hi, 256)]

    D = block(0)
    jobs = []
    for k in range(NB):
        ((L, W),) = run([chol128(D)], jobs)
        W3 = cut3(W)
        n = panel_rows(k)
        panels[k][0:B, :] = L
        jobs = []
        start = B
        if k + 1 < NB:
            top = times3([(cut3(base(k, B, 2 * B) if k == 0 else panels[k][B : 2 * B, :]), W3)])
            top3 = cut3(top)
            start = 2 * B
            pairs = [(top3, top3)]
            if k % 2 == 1:
                before = cuts[k - 1][2 * B : 3 * B, :]
                pairs.append((before, before))
            D = (block(k + 1) if k < 2 else panels[k + 1][0:B, :]) - times3(pairs)
            panels[k][B : 2 * B, :] = top
            cuts[k][B : 2 * B, :] = top3
        jobs += [solve(k, W3, lo, hi) for lo, hi in spans(start, n)]
        if k + 1 < NB:
            if k % 2 == 0:
                jobs += [update(k + 1, lo, hi, [k]) for lo, hi in spans(B, panel_rows(k + 1))]
            else:
                for j in range(k + 1, NB):
                    jobs += [update(j, lo, hi, [k - 1, k]) for lo, hi in spans(B if j == k + 1 else 0, panel_rows(j))]
        if k % 2 == 1:
            jobs += [gather([k - 1, k], 0), gather([k - 1, k], B)]
    for job in jobs:
        job()
    r0 = row0_ref[0]
    b = r0 // B
    off = r0 - b * B
    own_ref[...] = jnp.zeros(own_ref.shape, F)
    for k, panel in enumerate(panels):
        @pl.when(b >= k)
        def _():
            own_ref[:, k * B : (k + 1) * B] = panel[pl.ds(pl.multiple_of((b - k) * B + off, 16), 16), :]


def node_factor(row0, s, diag, coupler):
    return pl.pallas_call(
        node_kernel,
        out_shape=[jax.ShapeDtypeStruct((16, 1024), F), jax.ShapeDtypeStruct((256, 256), F)],
        in_specs=[pl.BlockSpec(memory_space=pltpu.SMEM)] + [VM] * 3,
        out_specs=[VM] * 2,
        scratch_shapes=[pltpu.VMEM((panel_rows(k), B), F) for k in range(NB)] + [pltpu.VMEM((panel_rows(k), 3 * B), jnp.bfloat16) for k in range(NB)],
        compiler_params=pltpu.CompilerParams(vmem_limit_bytes=24 << 20),
        cost_estimate=pl.CostEstimate(flops=1 << 33, bytes_accessed=8 << 20, transcendentals=1 << 14),
        name="node_factor",
    )(row0, s, diag, coupler)


def tail_kernel(s_ref, diag_ref, c_ref, od_ref, pf_ref, rf_ref):
    d0 = [s_ref[p, 0:B, :] + diag_mat(diag_ref[p : p + 1, 0:B]) for p in range(2)]
    r0 = run([chol128_halves(d) for d in d0])
    l10, lb0, d1, parts = [], [], [], []
    for p in range(2):
        L, W = r0[p]
        l10.append(dnt(s_ref[p, B : 2 * B, :], W))
        d1.append(s_ref[p, 2 * B :, :] + diag_mat(diag_ref[p : p + 1, B:]) - dnt(l10[p], l10[p]))
        pf_ref[p, 0:B, 0:B] = L
        pf_ref[p, 0:B, B:] = jnp.zeros((B, B), F)
        pf_ref[p, B:, 0:B] = l10[p]

    def early(p):
        def job():
            lb0.append(dnt(c_ref[p, 0:B, :].astype(F).T, r0[p][1]))
            parts.append((c_ref[p, B:, :].astype(F).T - dnt(lb0[p], l10[p]), dnt(lb0[p], lb0[p])))
        return job

    r1 = run([chol128_halves(d) for d in d1], [early(0), early(1)])
    root = diag_mat(od_ref[...])
    for p in range(2):
        L, W = r1[p]
        pf_ref[p, B:, B:] = L
        lb1 = dnt(parts[p][0], W)
        root = root + parts[p][1] + dnt(lb1, lb1)
    ((L, _),) = run([chol128(root)])
    rf_ref[...] = L


def tail(s, diag, coupler, od):
    return pl.pallas_call(
        tail_kernel,
        out_shape=[jax.ShapeDtypeStruct((2, 256, 256), F), jax.ShapeDtypeStruct((128, 128), F)],
        in_specs=[VM] * 4,
        out_specs=[VM] * 2,
        compiler_params=pltpu.CompilerParams(vmem_limit_bytes=24 << 20),
        cost_estimate=pl.CostEstimate(flops=1 << 30, bytes_accessed=2 << 20, transcendentals=1 << 14),
        name="tail",
    )(s, diag, coupler, od)
def split(r, parts):
    return r.reshape(parts, r.shape[0] // parts, 128)


def added(r, axis, parts):
    return split(lax.all_to_all(r, axis, 0, 0, tiled=True), parts).sum(0)


def everywhere(r, axis, parts):
    copies = jnp.broadcast_to(r[None], (parts,) + r.shape).reshape(parts * r.shape[0], 128)
    return lax.all_to_all(copies, axis, 0, 0, tiled=True)


def per_device(samples, weights, pattern, diag, coupler, diag2, coupler2, diag3):
    s = schur(samples, weights, pattern)
    s = added(s, "x", 4)
    s = added(s, "zl", 4)
    s = split(lax.all_gather(s, "zh", axis=0, tiled=True), 4).sum(0)
    s = lax.all_gather(s, "zl", axis=0, tiled=True)
    row0 = ((lax.axis_index(("zh", "zl")) * 4 + lax.axis_index("x")) * 16).reshape(1).astype(jnp.int32)
    s, row0 = lax.optimization_barrier((s, row0))
    s = everywhere(s, "x", 4)
    own, cond = node_factor(row0, s, diag, coupler)
    low = jnp.concatenate([cond[:B, :B], cond[B:, :B], cond[B:, B:]], 0)
    low = low + lax.ppermute(low, "core", [(0, 1), (1, 0)])
    low = lax.all_gather(low, "y", axis=0).reshape(2, 2, 3 * B, B).sum(1)
    parent, root = tail(low, diag2, coupler2, diag3[None])
    return own[None], parent, root


def solution(mesh):
    devices = mesh.devices.reshape(4, 2, 4, 4, 4)
    finer = Mesh(devices, ("y", "core", "zh", "zl", "x"))
    node, scen = ("y", "core"), ("zh", "zl", "x")
    return jax.shard_map(
        per_device,
        mesh=finer,
        in_specs=(P(node + scen, None, None), P(node + scen, None), P(node + scen, None), P(node, None), P(node, None, None), P(), P(), P()),
        out_specs=(P(node, scen, None), P(), P()),
        check_vma=False,
    )
```
